128 devices in a mesh: row: 8 (over y, x_lo), col: 16 (over z, x_hi, core).
Axes of the slice: x: 4 (x_hi: 2, x_lo: 2; x = x_hi * 2 + x_lo), y: 4, z: 4, core: 2. Of those that a mesh axis runs over, the one named last changes fastest.
Arguments:
- blocks: bfloat16 [512, 32, 128, 128], P('row', 'col'), may hold values from -1.1953125 to 1.1953125
- columns: int32 [512, 32], replicated, may hold values from 0 to 31, as said below
Outputs:
- product: float32 [512, 32, 128, 128], P('row', 'col')
The draws below stay inside these ranges and needn't reach their ends.
Inputs may be any that keep to these rules, and one draw needn't show every extreme that they name: `columns`: in every panel each block row and each block column holds exactly 2 nonzero blocks; the 2 column indices of one row within one panel are distinct.
All inputs are finite; a program needn't handle non-finite values.
Results may differ from the reference program's by a relative error of at most 0.0003.
Values may be sent and summed in bfloat16 or wider, within the bound.
A program may use at most 192 MiB of HBM per device.

```python
import jax
import jax.numpy as jnp
from jax import lax

BS = 128
PB = 32
F = 2
STEPS = 3
NP = 16


def draw_columns(key, part):
    key = jax.random.fold_in(key, 7)
    panel_keys = jax.random.split(key, NP)
    orders = jax.vmap(lambda single: jax.random.permutation(single, PB))(panel_keys).astype(jnp.int32)
    filler = jnp.broadcast_to(jnp.arange(PB, dtype=jnp.int32), (NP, PB))
    places = jnp.zeros((NP, PB), jnp.int32).at[jnp.arange(NP)[:, None], orders].set(filler)
    rotation = jax.random.randint(jax.random.fold_in(key, 1), (NP, PB, NP, 1), 0, F)
    offsets = (jnp.arange(F, dtype=jnp.int32)[None, None, None, :] + rotation) % F
    spots = (places[:, :, None, None] + offsets) % PB
    result = orders[jnp.arange(NP)[None, None, :, None], spots]
    return result.reshape(NP * PB, NP * F).astype(jnp.int32)


def levels(rng, dims, cuts, low, largest):
    factor_of = 1.0
    for position, parts in cuts:
        steps = jax.random.uniform(jax.random.fold_in(jax.random.fold_in(rng, 6), position), (parts,), jnp.float32, low / len(cuts), largest / len(cuts))
        factor_of = factor_of * jnp.repeat(jnp.exp(steps), dims[position] // parts).reshape((-1,) + (1,) * (len(dims) - 1 - position))
    return factor_of


def bell_draw(key, dims, deviation, most, pieces=(), kind=jnp.bfloat16):
    array = deviation * jax.random.normal(key, dims, jnp.float32)
    if pieces:
        array = array * levels(key, dims, pieces, -0.22, 0.18)
    return jnp.clip(array, -most, most).astype(kind)


def setup_inputs(seed: int = 0) -> dict:
    seeds = jax.random.split(jax.random.key(seed), 3)
    blocks = bell_draw(seeds[0], (NP * PB, NP * F, BS, BS), 0.2, 1.1953125, ((0, 8), (1, 16)))
    columns = draw_columns(jax.random.fold_in(seeds[2], 71), 0)
    return {"blocks": blocks, "columns": columns}


def panel_product(left_blocks, left_cols, right_blocks, right_cols, target_cols):
    picked = jnp.take(right_blocks, left_cols, axis=0)
    picked_cols = jnp.take(right_cols, left_cols, axis=0)
    matches = (picked_cols[:, None, :, :] == target_cols[:, :, None, None]).astype(jnp.float32)
    chosen = jnp.einsum("refg,rfgxz->refxz", matches, picked.astype(jnp.float32), precision=lax.Precision.HIGHEST)
    return jnp.einsum("rfxy,refyz->rexz", left_blocks.astype(jnp.float32), chosen, precision=lax.Precision.HIGHEST)


def reference(blocks, columns):
    grid = blocks.reshape(NP, PB, NP, F, BS, BS)
    pattern = columns.reshape(NP, PB, NP, F)
    panel_ids = jnp.arange(NP, dtype=jnp.int32)

    def one_panel_row(panel_row):
        target = jnp.transpose(pattern[panel_row], (1, 0, 2))
        running = jnp.zeros((NP, PB, F, BS, BS), jnp.float32)
        for step_index in range(STEPS):
            inner_panel = (panel_row + panel_ids + step_index) % NP
            left_blocks = grid[panel_row, :, inner_panel]
            left_cols = pattern[panel_row, :, inner_panel]
            right_blocks = grid[inner_panel, :, panel_ids]
            right_cols = pattern[inner_panel, :, panel_ids]
            running = running + jax.vmap(panel_product)(left_blocks, left_cols, right_blocks, right_cols, target)
        return running

    stacked = lax.map(one_panel_row, panel_ids)
    return jnp.transpose(stacked, (0, 2, 1, 3, 4, 5)).reshape(NP * PB, NP * F, BS, BS)
```

```python
import jax
import jax.numpy as jnp
from jax import lax
from jax.experimental import pallas as pl
from jax.experimental.pallas import tpu as pltpu
from jax.sharding import PartitionSpec as P

STEPS = 3
PB = 32
BS = 128
MESH = pl.DeviceIdType.MESH


def kernel(rows_n, cols_n, pattern, own, out, left, right0, right1, right2, right3, total, left_recv, right_recv, send_sem, out_sem):
    rights = (right0, right1, right2, right3)
    r = lax.axis_index("row")
    c = lax.axis_index("col")
    chips = cols_n // 2
    m = c // 2
    core = c % 2

    barrier = pltpu.get_barrier_semaphore()
    for step in range(1, cols_n):
        pl.semaphore_signal(barrier, inc=1, device_id=(r, (c + step) % cols_n), device_id_type=MESH)
    for step in range(1, rows_n):
        pl.semaphore_signal(barrier, inc=1, device_id=((r + step) % rows_n, c), device_id_type=MESH)
    pl.semaphore_wait(barrier, cols_n + rows_n - 2)

    def panel(member):
        return own.at[pl.ds(pl.multiple_of(member * PB, PB), PB)]

    def remote(source, target, arrived, index, device):
        return pltpu.make_async_remote_copy(
            src_ref=source, dst_ref=target, send_sem=send_sem.at[index], recv_sem=arrived,
            device_id=device, device_id_type=MESH,
        )

    sends = []

    def send(source, target, arrived, index, device):
        here = jnp.logical_and(device[0] == r, device[1] == c)

        @pl.when(here)
        def _():
            pltpu.make_async_copy(source, target, arrived).start()

        @pl.when(jnp.logical_not(here))
        def _():
            remote(source, target, arrived, index, device).start()

        sends.append((source, target, arrived, index, device, here))

    def chip_col(shift, which):
        return ((m - shift + 2 * chips) % chips) * 2 + which

    late = 1 - core
    first_slot = jnp.where(core == 0, 5, 3)
    plan = (
        (1, r + 2 * late, 1 - core, first_slot),
        (0, r, core, 0),
        (1, r + 1, core, 4),
        (0, r + 1, core, 2),
    )
    for index, (member, shift, which, slot) in enumerate(plan):
        send(panel(member), left.at[slot], left_recv.at[slot], index, (r, chip_col(shift, which)))
    for j in range(4):
        member = (c + j) % 2
        dest = ((2 * r + member - c - j + 4 * rows_n) // 2) % rows_n
        send(panel(member), rights[j], right_recv.at[j], 4 + j, (dest, c))

    def wait(target, arrived):
        pltpu.make_async_copy(target, target, arrived).wait()

    other = (r, c + 1 - 2 * core)
    outer = jnp.where(core == 0, 2, 0)
    relays = []
    for index, (source, target) in enumerate(((outer, 1), (4, 3 + 2 * core))):
        wait(left.at[source], left_recv.at[source])
        copy = remote(left.at[source], left.at[target], left_recv.at[target], 8 + index, other)
        copy.start()
        relays.append(copy)
    for slot in (2 - outer, 1, 3, 5):
        wait(left.at[slot], left_recv.at[slot])
    for j in range(4):
        wait(rights[j], right_recv.at[j])

    for member in range(2):
        panel_row = 2 * r + member

        def row(a, carry, member=member, panel_row=panel_row):
            line = panel_row * PB + a
            goals = [pattern[line, 2 * c + e] for e in range(2)]
            acc = jnp.zeros((BS, 2 * BS), jnp.float32)
            for step in range(STEPS):
                inner = (panel_row + c + step) % cols_n
                block = right_rows = rights[member + step]
                slot = member * STEPS + step
                lhs = jnp.concatenate([left[slot, a, 0], left[slot, a, 1]], axis=1)
                parts = []
                for f in range(2):
                    pick = pattern[line, 2 * inner + f]
                    held = [pattern[inner * PB + pick, 2 * c + g] for g in range(2)]
                    blocks = [block[pick, g] for g in range(2)]
                    zero = jnp.zeros_like(blocks[0])
                    parts.append(jnp.concatenate(
                        [jnp.where(held[0] == goals[e], blocks[0], jnp.where(held[1] == goals[e], blocks[1], zero)) for e in range(2)],
                        axis=1))
                acc = acc + jnp.dot(lhs, jnp.concatenate(parts, axis=0), preferred_element_type=jnp.float32)
            total[member * PB + a, 0] = acc[:, :BS]
            total[member * PB + a, 1] = acc[:, BS:]
            return carry

        lax.fori_loop(0, PB, row, 0)
        half = pl.ds(member * PB, PB)
        pltpu.make_async_copy(total.at[half], out.at[half], out_sem.at[member]).start()

    for source, target, arrived, index, device, here in sends:
        @pl.when(jnp.logical_not(here))
        def _(args=(source, target, arrived, index, device)):
            remote(*args).wait_send()
    for copy in relays:
        copy.wait_send()
    for member in range(2):
        half = pl.ds(member * PB, PB)
        pltpu.make_async_copy(total.at[half], out.at[half], out_sem.at[member]).wait()


def solution(mesh):
    rows_n, cols_n = mesh.shape["row"], mesh.shape["col"]

    def shards(blocks, columns):
        panel = pltpu.VMEM((PB, 2, BS, BS), jnp.bfloat16)

        def body(*refs):
            kernel(rows_n, cols_n, *refs)

        return pl.pallas_call(
            body,
            out_shape=jax.ShapeDtypeStruct(blocks.shape, jnp.float32),
            in_specs=[pl.BlockSpec(memory_space=pltpu.SMEM), pl.BlockSpec(memory_space=pl.ANY)],
            out_specs=pl.BlockSpec(memory_space=pl.ANY),
            scratch_shapes=[
                pltpu.VMEM((6, PB, 2, BS, BS), jnp.bfloat16),
                panel, panel, panel, panel,
                pltpu.VMEM((2 * PB, 2, BS, BS), jnp.float32),
                pltpu.SemaphoreType.DMA((6,)),
                pltpu.SemaphoreType.DMA((4,)),
                pltpu.SemaphoreType.DMA((10,)),
                pltpu.SemaphoreType.DMA((2,)),
            ],
            compiler_params=pltpu.CompilerParams(
                collective_id=0, has_side_effects=True, vmem_limit_bytes=56 * 2**20
            ),
        )(columns, blocks)

    return jax.shard_map(
        shards, mesh=mesh, in_specs=(P("row", "col", None, None), P()),
        out_specs=P("row", "col", None, None), check_vma=False,
    )
```

```python
import jax
import jax.numpy as jnp
from jax import lax
from jax.experimental import pallas as pl
from jax.experimental.pallas import tpu as pltpu
from jax.sharding import PartitionSpec as P

STEPS = 3
PB = 32
BS = 128
CHUNKS = 8
CR = PB // CHUNKS
MESH = pl.DeviceIdType.MESH

CHAIN_LEFT = ((2952, 152), (400, 9824))
CHAIN_RIGHT = ((356, 2184), (2208, 8800))


def bit(masks, parity, member, position, core):
    mask = jnp.where(parity == 0, masks[0][member], masks[1][member])
    return jnp.bitwise_and(jnp.right_shift(mask, position * 2 + core), 1) == 1


def near_far(start):
    return start + start % 2, start + 1 - start % 2


class Way:
    def __init__(self, r, m, core, member, rows_n, chips):
        start = r + (1 - core) if member == 1 else r
        self.left = []
        for shift in near_far(start):
            rel = 2 * (shift - r) + core
            which = core if member == 0 else rel // 3
            self.left.append((shift, (r, ((m - shift + 2 * chips) % chips) * 2 + which), 3 * member + rel - member - which))
        start = m + core if member == 0 else m
        self.right = []
        for shift in near_far(start):
            self.right.append((shift, ((r - shift + 2 * rows_n) % rows_n, 2 * m + core), 2 * (shift - m) + member - core))
        self.chain_left = bit(CHAIN_LEFT, m % 2, member, r, core)
        self.chain_right = bit(CHAIN_RIGHT, r % 2, member, m, core)
        self.shared = jnp.logical_not(jnp.logical_or(self.chain_left, self.chain_right))


def kernel(rows_n, cols_n, pattern, own, out, left, right, relay, total, left_recv, right_recv, relay_recv, send_sem, out_sem):
    r = lax.axis_index("row")
    c = lax.axis_index("col")
    chips = cols_n // 2
    m = c // 2
    core = c % 2

    barrier = pltpu.get_barrier_semaphore()
    for step in range(1, cols_n):
        pl.semaphore_signal(barrier, inc=1, device_id=(r, (c + step) % cols_n), device_id_type=MESH)
    for step in range(1, rows_n):
        pl.semaphore_signal(barrier, inc=1, device_id=((r + step) % rows_n, c), device_id_type=MESH)
    partner = r + 1 - 2 * (r % 2)
    for step in range(1, cols_n):
        pl.semaphore_signal(barrier, inc=1, device_id=(partner, (c + step) % cols_n), device_id_type=MESH)
    pl.semaphore_wait(barrier, 2 * cols_n + rows_n - 3)

    def rows_of(chunk, base=0):
        return pl.ds(pl.multiple_of(base + chunk * CR, CR), CR)

    def own_part(member, chunk):
        return own.at[rows_of(chunk, member * PB)]

    def left_part(slot, chunk):
        return left.at[slot, rows_of(chunk)]

    def right_part(slot, chunk):
        return right.at[slot, rows_of(chunk)]

    def relay_part(member, chunk):
        return relay.at[member, rows_of(chunk)]

    def remote(source, target, arrived, flow, device):
        return pltpu.make_async_remote_copy(
            src_ref=source, dst_ref=target, send_sem=send_sem.at[flow], recv_sem=arrived,
            device_id=device, device_id_type=MESH,
        )

    def is_here(device):
        return jnp.logical_and(device[0] == r, device[1] == c)

    def send(source, target, arrived, flow, device):
        here = is_here(device)

        @pl.when(here)
        def _():
            pltpu.make_async_copy(source, target, arrived).start()

        @pl.when(jnp.logical_not(here))
        def _():
            remote(source, target, arrived, flow, device).start()

    def send_left(source, way, far, chunk, flow):
        _, device, slot = way.left[far]
        send(source, left_part(slot, chunk), left_recv.at[slot, chunk], flow, device)

    def send_right(source, way, far, chunk, flow):
        _, device, slot = way.right[far]
        send(source, right_part(slot, chunk), right_recv.at[slot, chunk], flow, device)

    def wait(part, arrived):
        pltpu.make_async_copy(part, part, arrived).wait()

    mine = [Way(r, m, core, member, rows_n, chips) for member in range(2)]
    passing = [Way(partner, m, core, member, rows_n, chips) for member in range(2)]
    near_left = []
    for member in range(2):
        home_core = core if member == 0 else jnp.where(r % 2 == 0, 1 - core, core)
        shift = near_far(r + (1 - home_core) if member == 1 else r)[0]
        near_left.append(Way(r, (m + shift) % chips, home_core, member, rows_n, chips))
    near_right = []
    for member in range(2):
        shift = near_far(m + core if member == 0 else m)[0]
        near_right.append(Way((r + shift) % rows_n, m, core, member, rows_n, chips))

    def flow(member, kind):
        return member * 9 + kind

    def first(chunk, carry):
        for member, way in enumerate(mine):
            source = own_part(member, chunk)

            @pl.when(way.shared)
            def _(member=member, source=source):
                remote(source, relay_part(member, chunk), relay_recv.at[member, chunk], flow(member, 0), (partner, c)).start()

            @pl.when(jnp.logical_and(way.chain_right, jnp.logical_not(way.chain_left)))
            def _(member=member, source=source, way=way):
                send_left(source, way, 1, chunk, flow(member, 3))

            @pl.when(jnp.logical_and(way.chain_left, jnp.logical_not(way.chain_right)))
            def _(member=member, source=source, way=way):
                send_right(source, way, 1, chunk, flow(member, 4))

            send_right(source, way, 0, chunk, flow(member, 1))
            send_left(source, way, 0, chunk, flow(member, 2))
        return carry

    lax.fori_loop(0, CHUNKS, first, 0)

    def onward(chunk, carry):
        for member, way in enumerate(passing):
            @pl.when(way.shared)
            def _(member=member, way=way):
                source = relay_part(member, chunk)
                wait(source, relay_recv.at[member, chunk])
                send_right(source, way, 1, chunk, flow(member, 5))
                send_left(source, way, 1, chunk, flow(member, 6))

        for member, way in enumerate(near_right):
            slot = way.right[0][2]
            wait(right_part(slot, chunk), right_recv.at[slot, chunk])

            @pl.when(way.chain_right)
            def _(member=member, way=way, slot=slot):
                send_right(right_part(slot, chunk), way, 1, chunk, flow(member, 8))

        for member, way in enumerate(near_left):
            slot = way.left[0][2]
            wait(left_part(slot, chunk), left_recv.at[slot, chunk])

            @pl.when(way.chain_left)
            def _(member=member, way=way, slot=slot):
                send_left(left_part(slot, chunk), way, 1, chunk, flow(member, 7))
        return carry

    lax.fori_loop(0, CHUNKS, onward, 0)

    sibling = (r, c + 1 - 2 * core)
    crossing = ((jnp.where(core == 0, 2, 0), 1), (4, 3 + 2 * core))
    arriving = jnp.where(core == 0, 3, 5)
    far_left = (2 * (1 - r % 2), jnp.where(r % 2 == 0, 4, arriving))

    def across(chunk, carry):
        for slot in far_left:
            wait(left_part(slot, chunk), left_recv.at[slot, chunk])
        for index, (source, target) in enumerate(crossing):
            remote(left_part(source, chunk), left_part(target, chunk), left_recv.at[target, chunk], 18 + index, sibling).start()
        return carry

    lax.fori_loop(0, CHUNKS, across, 0)

    def arrived_right(chunk, carry):
        for way in near_right:
            slot = (way.right[0][2] + 2) % 4
            wait(right_part(slot, chunk), right_recv.at[slot, chunk])
        return carry

    lax.fori_loop(0, CHUNKS, arrived_right, 0)

    def multiply(chunk, carry):
        for slot in (1, 8 - arriving):
            wait(left_part(slot, chunk), left_recv.at[slot, chunk])
        for member in range(2):
            panel_row = 2 * r + member

            def row(step_row, carry, member=member, panel_row=panel_row):
                a = chunk * CR + step_row
                line = panel_row * PB + a
                goals = [pattern[line, 2 * c + e] for e in range(2)]
                acc = jnp.zeros((BS, 2 * BS), jnp.float32)
                for step in range(STEPS):
                    inner = (panel_row + c + step) % cols_n
                    slot = member * STEPS + step
                    lhs = jnp.concatenate([left[slot, a, 0], left[slot, a, 1]], axis=1)
                    parts = []
                    for f in range(2):
                        pick = pattern[line, 2 * inner + f]
                        held = [pattern[inner * PB + pick, 2 * c + g] for g in range(2)]
                        blocks = [right[member + step, pick, g] for g in range(2)]
                        zero = jnp.zeros_like(blocks[0])
                        parts.append(jnp.concatenate(
                            [jnp.where(held[0] == goals[e], blocks[0], jnp.where(held[1] == goals[e], blocks[1], zero)) for e in range(2)],
                            axis=1))
                    acc = acc + jnp.dot(lhs, jnp.concatenate(parts, axis=0), preferred_element_type=jnp.float32)
                total[member * PB + a, 0] = acc[:, :BS]
                total[member * PB + a, 1] = acc[:, BS:]
                return carry

            lax.fori_loop(0, CR, row, 0)
            part = rows_of(chunk, member * PB)
            pltpu.make_async_copy(total.at[part], out.at[part], out_sem.at[member]).start()
        return carry

    lax.fori_loop(0, CHUNKS, multiply, 0)

    def sent(number, condition):
        @pl.when(condition)
        def _():
            remote(left.at[0], left.at[0], left_recv.at[0, 0], number, sibling).wait_send()

    def away(device):
        return jnp.logical_not(is_here(device))

    for member in range(2):
        way, via = mine[member], passing[member]
        lonely_left = jnp.logical_and(way.chain_left, jnp.logical_not(way.chain_right))
        lonely_right = jnp.logical_and(way.chain_right, jnp.logical_not(way.chain_left))
        sent(flow(member, 0), way.shared)
        sent(flow(member, 1), away(way.right[0][1]))
        sent(flow(member, 2), away(way.left[0][1]))
        sent(flow(member, 3), jnp.logical_and(lonely_right, away(way.left[1][1])))
        sent(flow(member, 4), jnp.logical_and(lonely_left, away(way.right[1][1])))
        sent(flow(member, 5), jnp.logical_and(via.shared, away(via.right[1][1])))
        sent(flow(member, 6), jnp.logical_and(via.shared, away(via.left[1][1])))
        sent(flow(member, 7), jnp.logical_and(near_left[member].chain_left, away(near_left[member].left[1][1])))
        sent(flow(member, 8), jnp.logical_and(near_right[member].chain_right, away(near_right[member].right[1][1])))
    for index in range(2):
        remote(left.at[0], left.at[0], left_recv.at[0, 0], 18 + index, sibling).wait_send()
    for member in range(2):
        half = pl.ds(member * PB, PB)
        pltpu.make_async_copy(total.at[half], out.at[half], out_sem.at[member]).wait()


def solution(mesh):
    rows_n, cols_n = mesh.shape["row"], mesh.shape["col"]

    def shards(blocks, columns):
        def body(*refs):
            kernel(rows_n, cols_n, *refs)

        return pl.pallas_call(
            body,
            out_shape=jax.ShapeDtypeStruct(blocks.shape, jnp.float32),
            in_specs=[pl.BlockSpec(memory_space=pltpu.SMEM), pl.BlockSpec(memory_space=pl.ANY)],
            out_specs=pl.BlockSpec(memory_space=pl.ANY),
            scratch_shapes=[
                pltpu.VMEM((6, PB, 2, BS, BS), jnp.bfloat16),
                pltpu.VMEM((4, PB, 2, BS, BS), jnp.bfloat16),
                pltpu.VMEM((2, PB, 2, BS, BS), jnp.bfloat16),
                pltpu.VMEM((2 * PB, 2, BS, BS), jnp.float32),
                pltpu.SemaphoreType.DMA((6, CHUNKS)),
                pltpu.SemaphoreType.DMA((4, CHUNKS)),
                pltpu.SemaphoreType.DMA((2, CHUNKS)),
                pltpu.SemaphoreType.DMA((20,)),
                pltpu.SemaphoreType.DMA((2,)),
            ],
            compiler_params=pltpu.CompilerParams(
                collective_id=0, has_side_effects=True, vmem_limit_bytes=56 * 2**20
            ),
        )(columns, blocks)

    return jax.shard_map(
        shards, mesh=mesh, in_specs=(P("row", "col", None, None), P()),
        out_specs=P("row", "col", None, None), check_vma=False,
    )
```

```python
import jax
import jax.numpy as jnp
from jax import lax
from jax.experimental import pallas as pl
from jax.experimental.pallas import tpu as pltpu
from jax.sharding import PartitionSpec as P

STEPS = 3
PB = 32
BS = 128
CHUNKS = 8
CR = PB // CHUNKS
LAG = 0
MESH = pl.DeviceIdType.MESH

CHAIN_LEFT = ((2952, 152), (400, 9824))
CHAIN_RIGHT = ((356, 2184), (2208, 8800))


def bit(masks, parity, member, position, core):
    mask = jnp.where(parity == 0, masks[0][member], masks[1][member])
    return jnp.bitwise_and(jnp.right_shift(mask, position * 2 + core), 1) == 1


def near_far(start):
    return start + start % 2, start + 1 - start % 2


class Way:
    def __init__(self, r, m, core, member, rows_n, chips):
        start = r + (1 - core) if member == 1 else r
        self.left = []
        for shift in near_far(start):
            rel = 2 * (shift - r) + core
            which = core if member == 0 else rel // 3
            self.left.append((shift, (r, ((m - shift + 2 * chips) % chips) * 2 + which), 3 * member + rel - member - which))
        start = m + core if member == 0 else m
        self.right = []
        for shift in near_far(start):
            self.right.append((shift, ((r - shift + 2 * rows_n) % rows_n, 2 * m + core), 2 * (shift - m) + member - core))
        self.chain_left = bit(CHAIN_LEFT, m % 2, member, r, core)
        self.chain_right = bit(CHAIN_RIGHT, r % 2, member, m, core)
        self.shared = jnp.logical_not(jnp.logical_or(self.chain_left, self.chain_right))


def kernel(rows_n, cols_n, pattern, own, total, left, right, relay, left_recv, right_recv, relay_recv, send_sem):
    r = lax.axis_index("row")
    c = lax.axis_index("col")
    chips = cols_n // 2
    m = c // 2
    core = c % 2

    barrier = pltpu.get_barrier_semaphore()
    for step in range(1, cols_n):
        pl.semaphore_signal(barrier, inc=1, device_id=(r, (c + step) % cols_n), device_id_type=MESH)
    for step in range(1, rows_n):
        pl.semaphore_signal(barrier, inc=1, device_id=((r + step) % rows_n, c), device_id_type=MESH)
    partner = r + 1 - 2 * (r % 2)
    for step in range(1, cols_n):
        pl.semaphore_signal(barrier, inc=1, device_id=(partner, (c + step) % cols_n), device_id_type=MESH)
    pl.semaphore_wait(barrier, 2 * cols_n + rows_n - 3)

    def rows_of(chunk, base=0):
        return pl.ds(pl.multiple_of(base + chunk * CR, CR), CR)

    def own_part(member, chunk):
        return own.at[rows_of(chunk, member * PB)]

    def left_part(slot, chunk):
        return left.at[slot, rows_of(chunk)]

    def right_part(slot, chunk):
        return right.at[slot, rows_of(chunk)]

    def relay_part(member, chunk):
        return relay.at[member, rows_of(chunk)]

    def remote(source, target, arrived, flow, device):
        return pltpu.make_async_remote_copy(
            src_ref=source, dst_ref=target, send_sem=send_sem.at[flow], recv_sem=arrived,
            device_id=device, device_id_type=MESH,
        )

    def is_here(device):
        return jnp.logical_and(device[0] == r, device[1] == c)

    def send(source, target, arrived, flow, device):
        here = is_here(device)

        @pl.when(here)
        def _():
            pltpu.make_async_copy(source, target, arrived).start()

        @pl.when(jnp.logical_not(here))
        def _():
            remote(source, target, arrived, flow, device).start()

    def send_left(source, way, far, chunk, flow):
        _, device, slot = way.left[far]
        send(source, left_part(slot, chunk), left_recv.at[slot, chunk], flow, device)

    def send_right(source, way, far, chunk, flow):
        _, device, slot = way.right[far]
        send(source, right_part(slot, chunk), right_recv.at[slot, chunk], flow, device)

    def wait(part, arrived):
        pltpu.make_async_copy(part, part, arrived).wait()

    mine = [Way(r, m, core, member, rows_n, chips) for member in range(2)]
    passing = [Way(partner, m, core, member, rows_n, chips) for member in range(2)]
    near_left = []
    for member in range(2):
        home_core = core if member == 0 else jnp.where(r % 2 == 0, 1 - core, core)
        shift = near_far(r + (1 - home_core) if member == 1 else r)[0]
        near_left.append(Way(r, (m + shift) % chips, home_core, member, rows_n, chips))
    near_right = []
    for member in range(2):
        shift = near_far(m + core if member == 0 else m)[0]
        near_right.append(Way((r + shift) % rows_n, m, core, member, rows_n, chips))

    def flow(member, kind):
        return member * 9 + kind

    def first(chunk, carry):
        for member, way in enumerate(mine):
            source = own_part(member, chunk)

            @pl.when(way.shared)
            def _(member=member, source=source):
                remote(source, relay_part(member, chunk), relay_recv.at[member, chunk], flow(member, 0), (partner, c)).start()

            @pl.when(jnp.logical_and(way.chain_right, jnp.logical_not(way.chain_left)))
            def _(member=member, source=source, way=way):
                send_left(source, way, 1, chunk, flow(member, 3))

            @pl.when(jnp.logical_and(way.chain_left, jnp.logical_not(way.chain_right)))
            def _(member=member, source=source, way=way):
                send_right(source, way, 1, chunk, flow(member, 4))

            send_right(source, way, 0, chunk, flow(member, 1))
            send_left(source, way, 0, chunk, flow(member, 2))
        return carry

    lax.fori_loop(0, CHUNKS, first, 0)

    def onward(chunk, carry):
        for member, way in enumerate(passing):
            @pl.when(way.shared)
            def _(member=member, way=way):
                source = relay_part(member, chunk)
                wait(source, relay_recv.at[member, chunk])
                send_right(source, way, 1, chunk, flow(member, 5))
                send_left(source, way, 1, chunk, flow(member, 6))

        @pl.when(chunk >= LAG)
        def _():
            chained(chunk - LAG)
        return carry

    def chained(chunk):
        for member, way in enumerate(near_right):
            @pl.when(way.chain_right)
            def _(member=member, way=way):
                slot = way.right[0][2]
                wait(right_part(slot, chunk), right_recv.at[slot, chunk])
                send_right(right_part(slot, chunk), way, 1, chunk, flow(member, 8))

        for member, way in enumerate(near_left):
            @pl.when(way.chain_left)
            def _(member=member, way=way):
                slot = way.left[0][2]
                wait(left_part(slot, chunk), left_recv.at[slot, chunk])
                send_left(left_part(slot, chunk), way, 1, chunk, flow(member, 7))

    lax.fori_loop(0, CHUNKS, onward, 0)
    for chunk in range(CHUNKS - LAG, CHUNKS):
        chained(chunk)

    def arrived_near(chunk, carry):
        for way in near_right:
            @pl.when(jnp.logical_not(way.chain_right))
            def _(way=way):
                slot = way.right[0][2]
                wait(right_part(slot, chunk), right_recv.at[slot, chunk])

        for way in near_left:
            @pl.when(jnp.logical_not(way.chain_left))
            def _(way=way):
                slot = way.left[0][2]
                wait(left_part(slot, chunk), left_recv.at[slot, chunk])
        return carry

    lax.fori_loop(0, CHUNKS, arrived_near, 0)

    sibling = (r, c + 1 - 2 * core)
    crossing = ((jnp.where(core == 0, 2, 0), 1), (4, 3 + 2 * core))
    arriving = jnp.where(core == 0, 3, 5)
    far_left = (2 * (1 - r % 2), jnp.where(r % 2 == 0, 4, arriving))

    def across(chunk, carry):
        for slot in far_left:
            wait(left_part(slot, chunk), left_recv.at[slot, chunk])
        for index, (source, target) in enumerate(crossing):
            remote(left_part(source, chunk), left_part(target, chunk), left_recv.at[target, chunk], 18 + index, sibling).start()
        return carry

    lax.fori_loop(0, CHUNKS, across, 0)

    def arrived_right(chunk, carry):
        for way in near_right:
            slot = (way.right[0][2] + 2) % 4
            wait(right_part(slot, chunk), right_recv.at[slot, chunk])
        return carry

    lax.fori_loop(0, CHUNKS, arrived_right, 0)

    def multiply(chunk, carry):
        for slot in (1, 8 - arriving):
            wait(left_part(slot, chunk), left_recv.at[slot, chunk])
        def row(step_row, carry):
            a = chunk * CR + step_row
            for member in range(2):
                panel_row = 2 * r + member
                line = panel_row * PB + a
                goals = [pattern[line, 2 * c + e] for e in range(2)]
                acc = jnp.zeros((BS, 2 * BS), jnp.float32)
                for step in range(STEPS):
                    inner = (panel_row + c + step) % cols_n
                    slot = member * STEPS + step
                    lhs = jnp.concatenate([left[slot, a, 0], left[slot, a, 1]], axis=1)
                    parts = []
                    for f in range(2):
                        pick = pattern[line, 2 * inner + f]
                        held = [pattern[inner * PB + pick, 2 * c + g] for g in range(2)]
                        blocks = [right[member + step, pick, g] for g in range(2)]
                        zero = jnp.zeros_like(blocks[0])
                        parts.append(jnp.concatenate(
                            [jnp.where(held[0] == goals[e], blocks[0], jnp.where(held[1] == goals[e], blocks[1], zero)) for e in range(2)],
                            axis=1))
                    acc = acc + jnp.dot(lhs, jnp.concatenate(parts, axis=0), preferred_element_type=jnp.float32)
                total[member * PB + a, 0] = acc[:, :BS]
                total[member * PB + a, 1] = acc[:, BS:]
            return carry

        lax.fori_loop(0, CR, row, 0, unroll=True)
        return carry

    lax.fori_loop(0, CHUNKS, multiply, 0)

    def sent(number, condition):
        @pl.when(condition)
        def _():
            remote(left.at[0], left.at[0], left_recv.at[0, 0], number, sibling).wait_send()

    def away(device):
        return jnp.logical_not(is_here(device))

    for member in range(2):
        way, via = mine[member], passing[member]
        lonely_left = jnp.logical_and(way.chain_left, jnp.logical_not(way.chain_right))
        lonely_right = jnp.logical_and(way.chain_right, jnp.logical_not(way.chain_left))
        sent(flow(member, 0), way.shared)
        sent(flow(member, 1), away(way.right[0][1]))
        sent(flow(member, 2), away(way.left[0][1]))
        sent(flow(member, 3), jnp.logical_and(lonely_right, away(way.left[1][1])))
        sent(flow(member, 4), jnp.logical_and(lonely_left, away(way.right[1][1])))
        sent(flow(member, 5), jnp.logical_and(via.shared, away(via.right[1][1])))
        sent(flow(member, 6), jnp.logical_and(via.shared, away(via.left[1][1])))
        sent(flow(member, 7), jnp.logical_and(near_left[member].chain_left, away(near_left[member].left[1][1])))
        sent(flow(member, 8), jnp.logical_and(near_right[member].chain_right, away(near_right[member].right[1][1])))
    for index in range(2):
        remote(left.at[0], left.at[0], left_recv.at[0, 0], 18 + index, sibling).wait_send()


def solution(mesh):
    rows_n, cols_n = mesh.shape["row"], mesh.shape["col"]

    def shards(blocks, columns):
        def body(*refs):
            kernel(rows_n, cols_n, *refs)

        return pl.pallas_call(
            body,
            out_shape=jax.ShapeDtypeStruct(blocks.shape, jnp.float32),
            in_specs=[pl.BlockSpec(memory_space=pltpu.SMEM), pl.BlockSpec(memory_space=pl.ANY)],
            out_specs=pl.BlockSpec(memory_space=pltpu.VMEM),
            scratch_shapes=[
                pltpu.VMEM((6, PB, 2, BS, BS), jnp.bfloat16),
                pltpu.VMEM((4, PB, 2, BS, BS), jnp.bfloat16),
                pltpu.VMEM((2, PB, 2, BS, BS), jnp.bfloat16),
                pltpu.SemaphoreType.DMA((6, CHUNKS)),
                pltpu.SemaphoreType.DMA((4, CHUNKS)),
                pltpu.SemaphoreType.DMA((2, CHUNKS)),
                pltpu.SemaphoreType.DMA((20,)),
            ],
            compiler_params=pltpu.CompilerParams(
                collective_id=0, has_side_effects=True, vmem_limit_bytes=40 * 2**20
            ),
        )(columns, blocks)

    return jax.shard_map(
        shards, mesh=mesh, in_specs=(P("row", "col", None, None), P()),
        out_specs=P("row", "col", None, None), check_vma=False,
    )
```

```python
import jax
import jax.numpy as jnp
from jax import lax
from jax.experimental import pallas as pl
from jax.experimental.pallas import tpu as pltpu
from jax.sharding import PartitionSpec as P

STEPS = 3
PB = 32
BS = 128
CHUNKS = 8
CR = PB // CHUNKS
LAG = 0
MESH = pl.DeviceIdType.MESH

CHAIN_LEFT = ((1092, 33688), (37264, 1360))
CHAIN_RIGHT = ((1092, 4948), (4496, 608))
TURN_LEFT = (((16, 0), (0, 0)), ((0, 0), (1024, 512)))
TURN_RIGHT = (((48, 0), (0, 0)), ((0, 0), (1024, 2304)))


def bit(masks, parity, member, position, core):
    mask = jnp.where(parity == 0, masks[0][member], masks[1][member])
    return jnp.bitwise_and(jnp.right_shift(mask, position * 2 + core), 1) == 1


def turn(masks, parity, member, position, core):
    return jnp.where(bit(masks[0], parity, member, position, core), 1, jnp.where(bit(masks[1], parity, member, position, core), -1, 0))


def halfway(start, end, around, direction):
    natural = 1 - 2 * (start % 2)
    opposite = (end - start + around) % around == around // 2
    return jnp.logical_and(opposite, direction == -natural), (start + direction + around) % around


def near_far(start):
    return start + start % 2, start + 1 - start % 2


class Way:
    def __init__(self, r, m, core, member, rows_n, chips):
        start = r + (1 - core) if member == 1 else r
        self.left = []
        for shift in near_far(start):
            rel = 2 * (shift - r) + core
            which = core if member == 0 else rel // 3
            self.left.append((shift, (r, ((m - shift + 2 * chips) % chips) * 2 + which), 3 * member + rel - member - which))
        start = m + core if member == 0 else m
        self.right = []
        for shift in near_far(start):
            self.right.append((shift, ((r - shift + 2 * rows_n) % rows_n, 2 * m + core), 2 * (shift - m) + member - core))
        self.chain_left = bit(CHAIN_LEFT, m % 2, member, r, core)
        self.chain_right = bit(CHAIN_RIGHT, r % 2, member, m, core)
        self.shared = jnp.logical_not(jnp.logical_or(self.chain_left, self.chain_right))
        far = self.left[1][1][1]
        stops, stop = halfway(m // 2, far // 4, chips // 2, turn(TURN_LEFT, m % 2, member, r, core))
        self.stop_left, self.left_stop = jnp.logical_and(self.shared, stops), (r, stop * 4 + far % 4)
        far = self.right[1][1][0]
        stops, stop = halfway(r // 2, far // 2, rows_n // 2, turn(TURN_RIGHT, r % 2, member, m, core))
        self.stop_right, self.right_stop = jnp.logical_and(self.shared, stops), (stop * 2 + far % 2, 2 * m + core)


def kernel(rows_n, cols_n, pattern, own, total, left, right, relay, stop_left, stop_right, left_recv, right_recv, relay_recv, stop_left_recv, stop_right_recv, send_sem):
    r = lax.axis_index("row")
    c = lax.axis_index("col")
    chips = cols_n // 2
    m = c // 2
    core = c % 2

    barrier = pltpu.get_barrier_semaphore()
    for step in range(1, cols_n):
        pl.semaphore_signal(barrier, inc=1, device_id=(r, (c + step) % cols_n), device_id_type=MESH)
    for step in range(1, rows_n):
        pl.semaphore_signal(barrier, inc=1, device_id=((r + step) % rows_n, c), device_id_type=MESH)
    partner = r + 1 - 2 * (r % 2)
    for step in range(1, cols_n):
        pl.semaphore_signal(barrier, inc=1, device_id=(partner, (c + step) % cols_n), device_id_type=MESH)
    pl.semaphore_wait(barrier, 2 * cols_n + rows_n - 3)

    def rows_of(chunk, base=0):
        return pl.ds(pl.multiple_of(base + chunk * CR, CR), CR)

    def own_part(member, chunk):
        return own.at[rows_of(chunk, member * PB)]

    def left_part(slot, chunk):
        return left.at[slot, rows_of(chunk)]

    def right_part(slot, chunk):
        return right.at[slot, rows_of(chunk)]

    def relay_part(member, chunk):
        return relay.at[member, rows_of(chunk)]

    def stop_part(buffer, member, chunk):
        return buffer.at[member, rows_of(chunk)]

    def remote(source, target, arrived, flow, device):
        return pltpu.make_async_remote_copy(
            src_ref=source, dst_ref=target, send_sem=send_sem.at[flow], recv_sem=arrived,
            device_id=device, device_id_type=MESH,
        )

    def is_here(device):
        return jnp.logical_and(device[0] == r, device[1] == c)

    def send(source, target, arrived, flow, device):
        here = is_here(device)

        @pl.when(here)
        def _():
            pltpu.make_async_copy(source, target, arrived).start()

        @pl.when(jnp.logical_not(here))
        def _():
            remote(source, target, arrived, flow, device).start()

    def send_left(source, way, far, chunk, flow):
        _, device, slot = way.left[far]
        send(source, left_part(slot, chunk), left_recv.at[slot, chunk], flow, device)

    def send_right(source, way, far, chunk, flow):
        _, device, slot = way.right[far]
        send(source, right_part(slot, chunk), right_recv.at[slot, chunk], flow, device)

    def wait(part, arrived):
        pltpu.make_async_copy(part, part, arrived).wait()

    mine = [Way(r, m, core, member, rows_n, chips) for member in range(2)]
    passing = [Way(partner, m, core, member, rows_n, chips) for member in range(2)]
    near_left = []
    for member in range(2):
        home_core = core if member == 0 else jnp.where(r % 2 == 0, 1 - core, core)
        shift = near_far(r + (1 - home_core) if member == 1 else r)[0]
        near_left.append(Way(r, (m + shift) % chips, home_core, member, rows_n, chips))
    near_right = []
    for member in range(2):
        shift = near_far(m + core if member == 0 else m)[0]
        near_right.append(Way((r + shift) % rows_n, m, core, member, rows_n, chips))

    stopping_left, stopping_right = [], []
    for member in range(2):
        home_core = core if member == 0 else jnp.where(r % 2 == 0, core, 1 - core)
        direction = turn(TURN_LEFT, 1 - m % 2, member, r, home_core)
        home = (m // 2 - direction + chips // 2) % (chips // 2) * 2 + 1 - m % 2
        stopping_left.append(Way(r, home, home_core, member, rows_n, chips))
        direction = turn(TURN_RIGHT, 1 - r % 2, member, m, core)
        home = (r // 2 - direction + rows_n // 2) % (rows_n // 2) * 2 + 1 - r % 2
        stopping_right.append(Way(home, m, core, member, rows_n, chips))

    def flow(member, kind):
        return member * 9 + kind

    def first(chunk, carry):
        for member, way in enumerate(mine):
            source = own_part(member, chunk)

            @pl.when(way.shared)
            def _(member=member, source=source):
                remote(source, relay_part(member, chunk), relay_recv.at[member, chunk], flow(member, 0), (partner, c)).start()

            @pl.when(jnp.logical_and(way.chain_right, jnp.logical_not(way.chain_left)))
            def _(member=member, source=source, way=way):
                send_left(source, way, 1, chunk, flow(member, 3))

            @pl.when(jnp.logical_and(way.chain_left, jnp.logical_not(way.chain_right)))
            def _(member=member, source=source, way=way):
                send_right(source, way, 1, chunk, flow(member, 4))

            send_right(source, way, 0, chunk, flow(member, 1))
            send_left(source, way, 0, chunk, flow(member, 2))
        return carry

    lax.fori_loop(0, CHUNKS, first, 0)

    def onward(chunk, carry):
        for member, way in enumerate(passing):
            @pl.when(way.shared)
            def _(member=member, way=way):
                source = relay_part(member, chunk)
                wait(source, relay_recv.at[member, chunk])

                @pl.when(way.stop_right)
                def _():
                    remote(source, stop_part(stop_right, member, chunk), stop_right_recv.at[member, chunk], flow(member, 5), way.right_stop).start()

                @pl.when(jnp.logical_not(way.stop_right))
                def _():
                    send_right(source, way, 1, chunk, flow(member, 5))

                @pl.when(way.stop_left)
                def _():
                    remote(source, stop_part(stop_left, member, chunk), stop_left_recv.at[member, chunk], flow(member, 6), way.left_stop).start()

                @pl.when(jnp.logical_not(way.stop_left))
                def _():
                    send_left(source, way, 1, chunk, flow(member, 6))

        chained(chunk)

        @pl.when(chunk >= LAG)
        def _():
            stopped(chunk - LAG)
        return carry

    def stopped(chunk):
        for member in range(2):
            way = stopping_right[member]

            @pl.when(way.stop_right)
            def _(member=member, way=way):
                source = stop_part(stop_right, member, chunk)
                wait(source, stop_right_recv.at[member, chunk])
                send_right(source, way, 1, chunk, 18 + member)

            way = stopping_left[member]

            @pl.when(way.stop_left)
            def _(member=member, way=way):
                source = stop_part(stop_left, member, chunk)
                wait(source, stop_left_recv.at[member, chunk])
                send_left(source, way, 1, chunk, 20 + member)

    def chained(chunk):
        for member, way in enumerate(near_right):
            @pl.when(way.chain_right)
            def _(member=member, way=way):
                slot = way.right[0][2]
                wait(right_part(slot, chunk), right_recv.at[slot, chunk])
                send_right(right_part(slot, chunk), way, 1, chunk, flow(member, 8))

        for member, way in enumerate(near_left):
            @pl.when(way.chain_left)
            def _(member=member, way=way):
                slot = way.left[0][2]
                wait(left_part(slot, chunk), left_recv.at[slot, chunk])
                send_left(left_part(slot, chunk), way, 1, chunk, flow(member, 7))

    lax.fori_loop(0, CHUNKS, onward, 0)
    for chunk in range(CHUNKS - LAG, CHUNKS):
        stopped(chunk)

    def arrived_near(chunk, carry):
        for way in near_right:
            @pl.when(jnp.logical_not(way.chain_right))
            def _(way=way):
                slot = way.right[0][2]
                wait(right_part(slot, chunk), right_recv.at[slot, chunk])

        for way in near_left:
            @pl.when(jnp.logical_not(way.chain_left))
            def _(way=way):
                slot = way.left[0][2]
                wait(left_part(slot, chunk), left_recv.at[slot, chunk])
        return carry

    lax.fori_loop(0, CHUNKS, arrived_near, 0)

    sibling = (r, c + 1 - 2 * core)
    crossing = ((jnp.where(core == 0, 2, 0), 1), (4, 3 + 2 * core))
    arriving = jnp.where(core == 0, 3, 5)
    far_left = (2 * (1 - r % 2), jnp.where(r % 2 == 0, 4, arriving))

    def across(chunk, carry):
        for slot in far_left:
            wait(left_part(slot, chunk), left_recv.at[slot, chunk])
        for index, (source, target) in enumerate(crossing):
            remote(left_part(source, chunk), left_part(target, chunk), left_recv.at[target, chunk], 22 + index, sibling).start()
        return carry

    lax.fori_loop(0, CHUNKS, across, 0)

    def arrived_right(chunk, carry):
        for way in near_right:
            slot = (way.right[0][2] + 2) % 4
            wait(right_part(slot, chunk), right_recv.at[slot, chunk])
        return carry

    lax.fori_loop(0, CHUNKS, arrived_right, 0)

    def multiply(chunk, carry):
        for slot in (1, 8 - arriving):
            wait(left_part(slot, chunk), left_recv.at[slot, chunk])
        def row(step_row, carry):
            a = chunk * CR + step_row
            for member in range(2):
                panel_row = 2 * r + member
                line = panel_row * PB + a
                goals = [pattern[line, 2 * c + e] for e in range(2)]
                acc = jnp.zeros((BS, 2 * BS), jnp.float32)
                for step in range(STEPS):
                    inner = (panel_row + c + step) % cols_n
                    slot = member * STEPS + step
                    lhs = jnp.concatenate([left[slot, a, 0], left[slot, a, 1]], axis=1)
                    parts = []
                    for f in range(2):
                        pick = pattern[line, 2 * inner + f]
                        held = [pattern[inner * PB + pick, 2 * c + g] for g in range(2)]
                        blocks = [right[member + step, pick, g] for g in range(2)]
                        zero = jnp.zeros_like(blocks[0])
                        parts.append(jnp.concatenate(
                            [jnp.where(held[0] == goals[e], blocks[0], jnp.where(held[1] == goals[e], blocks[1], zero)) for e in range(2)],
                            axis=1))
                    acc = acc + jnp.dot(lhs, jnp.concatenate(parts, axis=0), preferred_element_type=jnp.float32)
                total[member * PB + a, 0] = acc[:, :BS]
                total[member * PB + a, 1] = acc[:, BS:]
            return carry

        lax.fori_loop(0, CR, row, 0, unroll=True)
        return carry

    lax.fori_loop(0, CHUNKS, multiply, 0)

    def sent(number, condition):
        @pl.when(condition)
        def _():
            remote(left.at[0], left.at[0], left_recv.at[0, 0], number, sibling).wait_send()

    def away(device):
        return jnp.logical_not(is_here(device))

    for member in range(2):
        way, via = mine[member], passing[member]
        lonely_left = jnp.logical_and(way.chain_left, jnp.logical_not(way.chain_right))
        lonely_right = jnp.logical_and(way.chain_right, jnp.logical_not(way.chain_left))
        sent(flow(member, 0), way.shared)
        sent(flow(member, 1), away(way.right[0][1]))
        sent(flow(member, 2), away(way.left[0][1]))
        sent(flow(member, 3), jnp.logical_and(lonely_right, away(way.left[1][1])))
        sent(flow(member, 4), jnp.logical_and(lonely_left, away(way.right[1][1])))
        sent(flow(member, 5), jnp.logical_and(via.shared, jnp.logical_or(via.stop_right, away(via.right[1][1]))))
        sent(flow(member, 6), jnp.logical_and(via.shared, jnp.logical_or(via.stop_left, away(via.left[1][1]))))
        sent(18 + member, stopping_right[member].stop_right)
        sent(20 + member, stopping_left[member].stop_left)
        sent(flow(member, 7), jnp.logical_and(near_left[member].chain_left, away(near_left[member].left[1][1])))
        sent(flow(member, 8), jnp.logical_and(near_right[member].chain_right, away(near_right[member].right[1][1])))
    for index in range(2):
        remote(left.at[0], left.at[0], left_recv.at[0, 0], 22 + index, sibling).wait_send()


def solution(mesh):
    rows_n, cols_n = mesh.shape["row"], mesh.shape["col"]

    def shards(blocks, columns):
        def body(*refs):
            kernel(rows_n, cols_n, *refs)

        return pl.pallas_call(
            body,
            out_shape=jax.ShapeDtypeStruct(blocks.shape, jnp.float32),
            in_specs=[pl.BlockSpec(memory_space=pltpu.SMEM), pl.BlockSpec(memory_space=pl.ANY)],
            out_specs=pl.BlockSpec(memory_space=pltpu.VMEM),
            scratch_shapes=[
                pltpu.VMEM((6, PB, 2, BS, BS), jnp.bfloat16),
                pltpu.VMEM((4, PB, 2, BS, BS), jnp.bfloat16),
                pltpu.VMEM((2, PB, 2, BS, BS), jnp.bfloat16),
                pltpu.VMEM((2, PB, 2, BS, BS), jnp.bfloat16),
                pltpu.VMEM((2, PB, 2, BS, BS), jnp.bfloat16),
                pltpu.SemaphoreType.DMA((6, CHUNKS)),
                pltpu.SemaphoreType.DMA((4, CHUNKS)),
                pltpu.SemaphoreType.DMA((2, CHUNKS)),
                pltpu.SemaphoreType.DMA((2, CHUNKS)),
                pltpu.SemaphoreType.DMA((2, CHUNKS)),
                pltpu.SemaphoreType.DMA((24,)),
            ],
            compiler_params=pltpu.CompilerParams(
                collective_id=0, has_side_effects=True, vmem_limit_bytes=36 * 2**20
            ),
        )(columns, blocks)

    return jax.shard_map(
        shards, mesh=mesh, in_specs=(P("row", "col", None, None), P()),
        out_specs=P("row", "col", None, None), check_vma=False,
    )
```

```python
import jax
import jax.numpy as jnp
from jax import lax
from jax.experimental import pallas as pl
from jax.experimental.pallas import tpu as pltpu
from jax.sharding import PartitionSpec as P

STEPS = 3
PB = 32
BS = 128
CHUNKS = 8
CR = PB // CHUNKS
LAG = 1
MESH = pl.DeviceIdType.MESH

CHAIN_LEFT = ((1092, 7065), (4496, 9826))
CHAIN_RIGHT = ((1092, 7064), (6545, 8804))
TURN_LEFT = (((16, 4), (0, 1)), ((0, 0), (1024, 2048)))
TURN_RIGHT = (((48, 16384), (0, 0)), ((0, 0), (1024, 0)))


def bit(masks, parity, member, position, core):
    mask = jnp.where(parity == 0, masks[0][member], masks[1][member])
    return jnp.bitwise_and(jnp.right_shift(mask, position * 2 + core), 1) == 1


def turn(masks, parity, member, position, core):
    return jnp.where(bit(masks[0], parity, member, position, core), 1, jnp.where(bit(masks[1], parity, member, position, core), -1, 0))


def halfway(start, end, around, direction):
    natural = 1 - 2 * (start % 2)
    opposite = (end - start + around) % around == around // 2
    return jnp.logical_and(opposite, direction == -natural), (start + direction + around) % around


def near_far(start):
    return start + start % 2, start + 1 - start % 2


class Way:
    def __init__(self, r, m, core, member, rows_n, chips):
        start = r + (1 - core) if member == 1 else r
        self.left = []
        for shift in near_far(start):
            rel = 2 * (shift - r) + core
            which = core if member == 0 else rel // 3
            self.left.append((shift, (r, ((m - shift + 2 * chips) % chips) * 2 + which), 3 * member + rel - member - which))
        start = m + core if member == 0 else m
        self.right = []
        for shift in near_far(start):
            self.right.append((shift, ((r - shift + 2 * rows_n) % rows_n, 2 * m + core), 2 * (shift - m) + member - core))
        self.chain_left = bit(CHAIN_LEFT, m % 2, member, r, core)
        self.chain_right = bit(CHAIN_RIGHT, r % 2, member, m, core)
        self.shared = jnp.logical_not(jnp.logical_or(self.chain_left, self.chain_right))
        far = self.left[1][1][1]
        stops, stop = halfway(m // 2, far // 4, chips // 2, turn(TURN_LEFT, m % 2, member, r, core))
        self.stop_left, self.left_stop = jnp.logical_and(self.shared, stops), (r, stop * 4 + far % 4)
        far = self.right[1][1][0]
        stops, stop = halfway(r // 2, far // 2, rows_n // 2, turn(TURN_RIGHT, r % 2, member, m, core))
        self.stop_right, self.right_stop = jnp.logical_and(self.shared, stops), (stop * 2 + far % 2, 2 * m + core)


def kernel(rows_n, cols_n, pattern, own, total, left, right, relay, stop_left, stop_right, left_recv, right_recv, relay_recv, stop_left_recv, stop_right_recv, send_sem):
    r = lax.axis_index("row")
    c = lax.axis_index("col")
    chips = cols_n // 2
    m = c // 2
    core = c % 2

    barrier = pltpu.get_barrier_semaphore()
    for step in range(1, cols_n):
        pl.semaphore_signal(barrier, inc=1, device_id=(r, (c + step) % cols_n), device_id_type=MESH)
    for step in range(1, rows_n):
        pl.semaphore_signal(barrier, inc=1, device_id=((r + step) % rows_n, c), device_id_type=MESH)
    partner = r + 1 - 2 * (r % 2)
    for step in range(1, cols_n):
        pl.semaphore_signal(barrier, inc=1, device_id=(partner, (c + step) % cols_n), device_id_type=MESH)
    pl.semaphore_wait(barrier, 2 * cols_n + rows_n - 3)

    def rows_of(chunk, base=0):
        return pl.ds(pl.multiple_of(base + chunk * CR, CR), CR)

    def own_part(member, chunk):
        return own.at[rows_of(chunk, member * PB)]

    def left_part(slot, chunk):
        return left.at[slot, rows_of(chunk)]

    def right_part(slot, chunk):
        return right.at[slot, rows_of(chunk)]

    def relay_part(member, chunk):
        return relay.at[member, rows_of(chunk)]

    def stop_part(buffer, member, chunk):
        return buffer.at[member, rows_of(chunk)]

    def remote(source, target, arrived, flow, device):
        return pltpu.make_async_remote_copy(
            src_ref=source, dst_ref=target, send_sem=send_sem.at[flow], recv_sem=arrived,
            device_id=device, device_id_type=MESH,
        )

    def is_here(device):
        return jnp.logical_and(device[0] == r, device[1] == c)

    def send(source, target, arrived, flow, device):
        here = is_here(device)

        @pl.when(here)
        def _():
            pltpu.make_async_copy(source, target, arrived).start()

        @pl.when(jnp.logical_not(here))
        def _():
            remote(source, target, arrived, flow, device).start()

    def send_left(source, way, far, chunk, flow):
        _, device, slot = way.left[far]
        send(source, left_part(slot, chunk), left_recv.at[slot, chunk], flow, device)

    def send_right(source, way, far, chunk, flow):
        _, device, slot = way.right[far]
        send(source, right_part(slot, chunk), right_recv.at[slot, chunk], flow, device)

    def wait(part, arrived):
        pltpu.make_async_copy(part, part, arrived).wait()

    mine = [Way(r, m, core, member, rows_n, chips) for member in range(2)]
    passing = [Way(partner, m, core, member, rows_n, chips) for member in range(2)]
    near_left = []
    for member in range(2):
        home_core = core if member == 0 else jnp.where(r % 2 == 0, 1 - core, core)
        shift = near_far(r + (1 - home_core) if member == 1 else r)[0]
        near_left.append(Way(r, (m + shift) % chips, home_core, member, rows_n, chips))
    near_right = []
    for member in range(2):
        shift = near_far(m + core if member == 0 else m)[0]
        near_right.append(Way((r + shift) % rows_n, m, core, member, rows_n, chips))

    stopping_left, stopping_right = [], []
    for member in range(2):
        home_core = core if member == 0 else jnp.where(r % 2 == 0, core, 1 - core)
        direction = turn(TURN_LEFT, 1 - m % 2, member, r, home_core)
        home = (m // 2 - direction + chips // 2) % (chips // 2) * 2 + 1 - m % 2
        stopping_left.append(Way(r, home, home_core, member, rows_n, chips))
        direction = turn(TURN_RIGHT, 1 - r % 2, member, m, core)
        home = (r // 2 - direction + rows_n // 2) % (rows_n // 2) * 2 + 1 - r % 2
        stopping_right.append(Way(home, m, core, member, rows_n, chips))

    def flow(member, kind):
        return member * 9 + kind

    def first(chunk, carry):
        for member, way in enumerate(mine):
            source = own_part(member, chunk)

            @pl.when(way.shared)
            def _(member=member, source=source):
                remote(source, relay_part(member, chunk), relay_recv.at[member, chunk], flow(member, 0), (partner, c)).start()

            @pl.when(jnp.logical_and(way.chain_right, jnp.logical_not(way.chain_left)))
            def _(member=member, source=source, way=way):
                send_left(source, way, 1, chunk, flow(member, 3))

            @pl.when(jnp.logical_and(way.chain_left, jnp.logical_not(way.chain_right)))
            def _(member=member, source=source, way=way):
                send_right(source, way, 1, chunk, flow(member, 4))

            send_right(source, way, 0, chunk, flow(member, 1))

            @pl.when(way.chain_left)
            def _(member=member, source=source, way=way):
                send_left(source, way, 0, chunk, flow(member, 2))
        return carry

    def second(chunk, carry):
        for member, way in enumerate(mine):
            source = own_part(member, chunk)

            @pl.when(jnp.logical_not(way.chain_left))
            def _(member=member, source=source, way=way):
                send_left(source, way, 0, chunk, flow(member, 2))
        return carry

    lax.fori_loop(0, CHUNKS, first, 0)
    lax.fori_loop(0, CHUNKS, second, 0)

    def onward(chunk, carry):
        for member, way in enumerate(passing):
            @pl.when(way.shared)
            def _(member=member, way=way):
                source = relay_part(member, chunk)
                wait(source, relay_recv.at[member, chunk])

                @pl.when(way.stop_right)
                def _():
                    remote(source, stop_part(stop_right, member, chunk), stop_right_recv.at[member, chunk], flow(member, 5), way.right_stop).start()

                @pl.when(jnp.logical_not(way.stop_right))
                def _():
                    send_right(source, way, 1, chunk, flow(member, 5))

                @pl.when(way.stop_left)
                def _():
                    remote(source, stop_part(stop_left, member, chunk), stop_left_recv.at[member, chunk], flow(member, 6), way.left_stop).start()

                @pl.when(jnp.logical_not(way.stop_left))
                def _():
                    send_left(source, way, 1, chunk, flow(member, 6))

        chained(chunk)

        @pl.when(chunk >= LAG)
        def _():
            stopped(chunk - LAG)
        return carry

    def stopped(chunk):
        for member in range(2):
            way = stopping_right[member]

            @pl.when(way.stop_right)
            def _(member=member, way=way):
                source = stop_part(stop_right, member, chunk)
                wait(source, stop_right_recv.at[member, chunk])
                send_right(source, way, 1, chunk, 18 + member)

            way = stopping_left[member]

            @pl.when(way.stop_left)
            def _(member=member, way=way):
                source = stop_part(stop_left, member, chunk)
                wait(source, stop_left_recv.at[member, chunk])
                send_left(source, way, 1, chunk, 20 + member)

    def chained(chunk):
        for member, way in enumerate(near_right):
            @pl.when(way.chain_right)
            def _(member=member, way=way):
                slot = way.right[0][2]
                wait(right_part(slot, chunk), right_recv.at[slot, chunk])
                send_right(right_part(slot, chunk), way, 1, chunk, flow(member, 8))

        for member, way in enumerate(near_left):
            @pl.when(way.chain_left)
            def _(member=member, way=way):
                slot = way.left[0][2]
                wait(left_part(slot, chunk), left_recv.at[slot, chunk])
                send_left(left_part(slot, chunk), way, 1, chunk, flow(member, 7))

    lax.fori_loop(0, CHUNKS, onward, 0)
    for chunk in range(CHUNKS - LAG, CHUNKS):
        stopped(chunk)

    def arrived_near(chunk, carry):
        for way in near_right:
            @pl.when(jnp.logical_not(way.chain_right))
            def _(way=way):
                slot = way.right[0][2]
                wait(right_part(slot, chunk), right_recv.at[slot, chunk])

        for way in near_left:
            @pl.when(jnp.logical_not(way.chain_left))
            def _(way=way):
                slot = way.left[0][2]
                wait(left_part(slot, chunk), left_recv.at[slot, chunk])
        return carry

    lax.fori_loop(0, CHUNKS, arrived_near, 0)

    sibling = (r, c + 1 - 2 * core)
    crossing = ((jnp.where(core == 0, 2, 0), 1), (4, 3 + 2 * core))
    arriving = jnp.where(core == 0, 3, 5)
    far_left = (2 * (1 - r % 2), jnp.where(r % 2 == 0, 4, arriving))

    def across(chunk, carry):
        for slot in far_left:
            wait(left_part(slot, chunk), left_recv.at[slot, chunk])
        for index, (source, target) in enumerate(crossing):
            remote(left_part(source, chunk), left_part(target, chunk), left_recv.at[target, chunk], 22 + index, sibling).start()
        return carry

    lax.fori_loop(0, CHUNKS, across, 0)

    def arrived_right(chunk, carry):
        for way in near_right:
            slot = (way.right[0][2] + 2) % 4
            wait(right_part(slot, chunk), right_recv.at[slot, chunk])
        return carry

    lax.fori_loop(0, CHUNKS, arrived_right, 0)

    def multiply(chunk, carry):
        for slot in (1, 8 - arriving):
            wait(left_part(slot, chunk), left_recv.at[slot, chunk])
        def row(step_row, carry):
            a = chunk * CR + step_row
            for member in range(2):
                panel_row = 2 * r + member
                line = panel_row * PB + a
                goals = [pattern[line, 2 * c + e] for e in range(2)]
                acc = jnp.zeros((BS, 2 * BS), jnp.float32)
                for step in range(STEPS):
                    inner = (panel_row + c + step) % cols_n
                    slot = member * STEPS + step
                    lhs = jnp.concatenate([left[slot, a, 0], left[slot, a, 1]], axis=1)
                    parts = []
                    for f in range(2):
                        pick = pattern[line, 2 * inner + f]
                        held = [pattern[inner * PB + pick, 2 * c + g] for g in range(2)]
                        blocks = [right[member + step, pick, g] for g in range(2)]
                        zero = jnp.zeros_like(blocks[0])
                        parts.append(jnp.concatenate(
                            [jnp.where(held[0] == goals[e], blocks[0], jnp.where(held[1] == goals[e], blocks[1], zero)) for e in range(2)],
                            axis=1))
                    acc = acc + jnp.dot(lhs, jnp.concatenate(parts, axis=0), preferred_element_type=jnp.float32)
                total[member * PB + a, 0] = acc[:, :BS]
                total[member * PB + a, 1] = acc[:, BS:]
            return carry

        lax.fori_loop(0, CR, row, 0, unroll=True)
        return carry

    lax.fori_loop(0, CHUNKS, multiply, 0)

    def sent(number, condition):
        @pl.when(condition)
        def _():
            remote(left.at[0], left.at[0], left_recv.at[0, 0], number, sibling).wait_send()

    def away(device):
        return jnp.logical_not(is_here(device))

    for member in range(2):
        way, via = mine[member], passing[member]
        lonely_left = jnp.logical_and(way.chain_left, jnp.logical_not(way.chain_right))
        lonely_right = jnp.logical_and(way.chain_right, jnp.logical_not(way.chain_left))
        sent(flow(member, 0), way.shared)
        sent(flow(member, 1), away(way.right[0][1]))
        sent(flow(member, 2), away(way.left[0][1]))
        sent(flow(member, 3), jnp.logical_and(lonely_right, away(way.left[1][1])))
        sent(flow(member, 4), jnp.logical_and(lonely_left, away(way.right[1][1])))
        sent(flow(member, 5), jnp.logical_and(via.shared, jnp.logical_or(via.stop_right, away(via.right[1][1]))))
        sent(flow(member, 6), jnp.logical_and(via.shared, jnp.logical_or(via.stop_left, away(via.left[1][1]))))
        sent(18 + member, stopping_right[member].stop_right)
        sent(20 + member, stopping_left[member].stop_left)
        sent(flow(member, 7), jnp.logical_and(near_left[member].chain_left, away(near_left[member].left[1][1])))
        sent(flow(member, 8), jnp.logical_and(near_right[member].chain_right, away(near_right[member].right[1][1])))
    for index in range(2):
        remote(left.at[0], left.at[0], left_recv.at[0, 0], 22 + index, sibling).wait_send()


def solution(mesh):
    rows_n, cols_n = mesh.shape["row"], mesh.shape["col"]

    def shards(blocks, columns):
        def body(*refs):
            kernel(rows_n, cols_n, *refs)

        return pl.pallas_call(
            body,
            out_shape=jax.ShapeDtypeStruct(blocks.shape, jnp.float32),
            in_specs=[pl.BlockSpec(memory_space=pltpu.SMEM), pl.BlockSpec(memory_space=pl.ANY)],
            out_specs=pl.BlockSpec(memory_space=pltpu.VMEM),
            scratch_shapes=[
                pltpu.VMEM((6, PB, 2, BS, BS), jnp.bfloat16),
                pltpu.VMEM((4, PB, 2, BS, BS), jnp.bfloat16),
                pltpu.VMEM((2, PB, 2, BS, BS), jnp.bfloat16),
                pltpu.VMEM((2, PB, 2, BS, BS), jnp.bfloat16),
                pltpu.VMEM((2, PB, 2, BS, BS), jnp.bfloat16),
                pltpu.SemaphoreType.DMA((6, CHUNKS)),
                pltpu.SemaphoreType.DMA((4, CHUNKS)),
                pltpu.SemaphoreType.DMA((2, CHUNKS)),
                pltpu.SemaphoreType.DMA((2, CHUNKS)),
                pltpu.SemaphoreType.DMA((2, CHUNKS)),
                pltpu.SemaphoreType.DMA((24,)),
            ],
            compiler_params=pltpu.CompilerParams(
                collective_id=0, has_side_effects=True, vmem_limit_bytes=36 * 2**20
            ),
        )(columns, blocks)

    return jax.shard_map(
        shards, mesh=mesh, in_specs=(P("row", "col", None, None), P()),
        out_specs=P("row", "col", None, None), check_vma=False,
    )
```
